1024 devices in a mesh: dp: 64 (over y, x), expert: 16 (over z, core).
Axes of the slice: x: 8, y: 8, z: 8, core: 2. Of those that a mesh axis runs over, the one named last changes fastest.
Arguments:
- tokens: bfloat16 [131072, 1024], P(('dp', 'expert')), may hold values from -6 to 6
- expert_ids: int32 [131072, 2], P(('dp', 'expert')), may hold values from 0 to 15, all different within a row; in each aligned block of 128 rows (0 to 127, 128 to 255, ...) at most 24 rows name the same one
- routing: float32 [131072, 2], P(('dp', 'expert')), may hold values from 0.2 to 1
- w_gate: bfloat16 [16, 1024, 384], P('expert', 'dp'), may hold values from -0.1875 to 0.1875
- w_up: bfloat16 [16, 1024, 384], P('expert', 'dp'), may hold values from -0.1875 to 0.1875
- w_down: bfloat16 [16, 1024, 384], P('expert', 'dp'), may hold values from -0.3125 to 0.3125
- grad_out: bfloat16 [131072, 1024], P(('dp', 'expert')), may hold values from -6 to 6
Outputs:
- output: bfloat16 [131072, 1024], P(('dp', 'expert'))
- token_grad: bfloat16 [131072, 1024], P(('dp', 'expert'))
- down_grad: float32 [16, 1024, 384], P('expert', 'dp')
The draws below stay inside these ranges and needn't reach their ends.
Inputs may be any that keep to these rules, and one draw needn't show every extreme that they name: `expert_ids`: the 2 experts of a token differ. Among the 128 tokens of one device no expert is named by more than 24 (token, choice) pairs, and in every draw some device names some expert exactly 24 times.
All inputs are finite; a program needn't handle non-finite values.
Results may differ from the reference program's by a relative error of at most 0.0065.
Values may be sent and summed in bfloat16 or wider, within the bound.
A program may use at most 32 MiB of HBM per device.

```python
import math
import jax
import jax.numpy as jnp
import numpy as np
from jax import lax

D = 1024
FF = 384
TOP = 2
TOK_DEV = 128
EXPERTS = 16
CAP = 24
TOKENS = 131072
N_DP = 64
N_EXPERT = 16


def levels(rng, extent, split, least, high):
    def one(position, blocks):
        draws = jax.random.uniform(jax.random.fold_in(jax.random.fold_in(rng, 6), position), (blocks,), jnp.float32, least / len(split), high / len(split))
        return jnp.repeat(jnp.exp(draws), extent[position] // blocks).reshape((-1,) + (1,) * (len(extent) - position - 1))

    factor_of = one(*split[0])
    for cut in split[1:]:
        factor_of = factor_of * one(*cut)
    return factor_of


def routed_block(key, own, number, rows, count, top, limit, skew):
    sequence = jax.random.permutation(key, count)
    crowded, common = shares(count, rows * top, limit, skew, True), shares(count, rows * top, limit, skew, False)
    places = jnp.arange(count)

    def named(lengths, offset_by):
        used = int((lengths > 0).sum())
        fixed = max(1, used // 4)
        shifted = fixed + (places - fixed + offset_by * (used - fixed)) % max(1, count - fixed)
        return jnp.zeros((count,), jnp.int32).at[sequence[jnp.where(places < fixed, places, shifted)]].set(jnp.asarray(lengths, jnp.int32))

    lengths = jnp.where(number % 4 == 0, named(crowded, number // 4), named(common, number - number // 4 - 1))
    mixed = jax.random.permutation(jax.random.fold_in(own, 3), count)
    giver, sink = mixed[0:count // 2 * 2:2], mixed[1:count // 2 * 2:2]
    slack = jnp.minimum(lengths[giver] - 1, limit - lengths[sink]) // 2
    slack = jnp.where((giver == sequence[0]) | (sink == sequence[0]) | (lengths[sink] == 0), 0, jnp.maximum(slack, 0))
    shifted = jax.random.randint(jax.random.fold_in(own, 4), (count // 2,), 0, 1 << 20) % (slack + 1)
    lengths = lengths.at[giver].add(-shifted).at[sink].add(shifted)
    labels = jnp.searchsorted(jnp.cumsum(lengths), jnp.arange(rows * top), side="right").astype(jnp.int32)
    table = labels.reshape(top, rows).T
    table = table[jax.random.permutation(jax.random.fold_in(own, 1), rows)]
    offset_by = jax.random.randint(jax.random.fold_in(own, 2), (rows, 1), 0, top)
    return jnp.take_along_axis(table, (jnp.arange(top)[None, :] + offset_by) % top, axis=1)


def shares(amount, total, limit, skew, full):
    loads = [(1 << 20) // math.isqrt(grade ** skew) + 1 for grade in range(1, amount + 1)]
    largest = limit if full else min(limit, max(-(-total // amount), total * loads[0] // sum(loads)))
    least = 1 if total - largest >= amount - 1 else 0
    holding, spare = [largest] + [least] * (amount - 1), total - largest - least * (amount - 1)
    while spare > 0:
        movable = [i for i in range(1, amount) if holding[i] < largest] or [i for i in range(1, amount) if holding[i] < limit]
        pool, left = sum([loads[i] for i in movable]), spare
        for i in movable:
            addition = min(limit - holding[i], max(1, left * loads[i] // pool), spare)
            holding[i] = holding[i] + addition
            spare = spare - addition
    return np.array(holding)


def bell_draw(rng, shape, scale, limit, cuts=(), held_as=jnp.bfloat16):
    drawn = scale * jax.random.normal(rng, shape, jnp.float32)
    if cuts:
        drawn = drawn * levels(rng, shape, cuts, -0.22, 0.18)
    return jnp.clip(drawn, -limit, limit).astype(held_as)


def setup_inputs(seed: int = 0) -> dict:
    keys = jax.random.split(jax.random.key(seed), 8)
    tokens = bell_draw(keys[0], (TOKENS, D), 1.0, 6.0, ((0, 1024),))
    expert_ids_keys = jax.random.split(jax.random.fold_in(keys[1], 1), TOKENS // TOK_DEV)
    expert_ids_turns = jax.random.permutation(jax.random.fold_in(keys[1], 3), TOKENS // TOK_DEV)
    expert_ids = jax.vmap(lambda own, number: routed_block(jax.random.fold_in(keys[1], 2), own, number, TOK_DEV, EXPERTS, TOP, CAP, 2))(expert_ids_keys, expert_ids_turns).reshape((TOKENS, TOP))
    routing = jnp.clip(0.2 + 0.8 * jax.random.uniform(keys[2], (TOKENS, TOP), jnp.float32) ** levels(keys[2], (TOKENS, TOP), ((0, 1024),), -0.2, 0.2), 0.2, 1.0)
    w_gate = bell_draw(keys[3], (EXPERTS, D, FF), D ** -0.5, 0.1875, ((0, 16), (1, 64)))
    w_up = bell_draw(keys[4], (EXPERTS, D, FF), D ** -0.5, 0.1875, ((0, 16), (1, 64)))
    w_down = bell_draw(keys[5], (EXPERTS, D, FF), FF ** -0.5, 0.3125, ((0, 16), (1, 64)))
    grad_out = bell_draw(keys[6], (TOKENS, D), 1.0, 6.0, ((0, 1024),))
    return {"tokens": tokens, "expert_ids": expert_ids, "routing": routing, "w_gate": w_gate, "w_up": w_up, "w_down": w_down, "grad_out": grad_out}


def forward_rows(row_data, gate_w, up_w, down_w):
    gate_pre = jnp.dot(row_data.astype(jnp.float32), gate_w.astype(jnp.float32))
    up_pre = jnp.dot(row_data.astype(jnp.float32), up_w.astype(jnp.float32))
    sigmoid_val = jax.nn.sigmoid(gate_pre)
    hidden = (gate_pre * sigmoid_val * up_pre).astype(jnp.bfloat16)
    expert_out = jnp.dot(hidden.astype(jnp.float32), down_w.astype(jnp.float32).T).astype(jnp.bfloat16)
    return gate_pre, up_pre, hidden, expert_out


def backward_rows(grad_rows, gate_pre, up_pre, gate_w, up_w, down_w):
    hidden_grad = jnp.dot(grad_rows.astype(jnp.float32), down_w.astype(jnp.float32))
    sigmoid_val = jax.nn.sigmoid(gate_pre)
    slope_val = sigmoid_val * (1.0 + gate_pre * (1.0 - sigmoid_val))
    gate_grad = (hidden_grad * up_pre * slope_val).astype(jnp.bfloat16)
    up_grad = (hidden_grad * gate_pre * sigmoid_val).astype(jnp.bfloat16)
    summed = jnp.dot(gate_grad.astype(jnp.float32), gate_w.astype(jnp.float32).T)
    summed = summed + jnp.dot(up_grad.astype(jnp.float32), up_w.astype(jnp.float32).T)
    return summed.astype(jnp.bfloat16)


def reference(tokens, expert_ids, routing, w_gate, w_up, w_down, grad_out):
    devices_all = N_DP * N_EXPERT
    pair_count = TOK_DEV * TOP
    chosen = expert_ids.reshape(devices_all, pair_count)
    onehot = (chosen[:, :, None] == jnp.arange(EXPERTS, dtype=jnp.int32)[None, None, :]).astype(jnp.int32)
    before = jnp.cumsum(onehot, axis=1) - onehot
    slot_index = jnp.sum(before * onehot, axis=2).astype(jnp.int32)
    device_row = jnp.arange(devices_all, dtype=jnp.int32)[:, None]
    slab_rows = devices_all * CAP
    flat_index = (chosen * slab_rows + device_row * CAP + slot_index).astype(jnp.int32)
    owner_row = (device_row * TOK_DEV + jnp.arange(pair_count, dtype=jnp.int32)[None, :] // TOP).astype(jnp.int32)
    slot_owner = jnp.full((EXPERTS * slab_rows,), TOKENS, jnp.int32).at[flat_index.reshape(-1)].set(owner_row.reshape(-1))
    slot_owner = slot_owner.reshape(EXPERTS, slab_rows)
    weight_slot = jnp.zeros((EXPERTS * slab_rows,), jnp.float32).at[flat_index.reshape(-1)].set(routing.reshape(-1))
    weight_slot = weight_slot.reshape(EXPERTS, slab_rows)
    zero_row = jnp.zeros((1, D), tokens.dtype)
    tokens_pad = jnp.concatenate([tokens, zero_row], axis=0)
    grads_pad = jnp.concatenate([grad_out, zero_row], axis=0)

    def per_expert(expert):
        owners = slot_owner[expert]
        row_data = tokens_pad[owners]
        scaled = (weight_slot[expert][:, None] * grads_pad[owners].astype(jnp.float32)).astype(jnp.bfloat16)
        gate_w = w_gate[expert]
        up_w = w_up[expert]
        down_w = w_down[expert]
        gate_pre, up_pre, hidden, expert_out = forward_rows(row_data, gate_w, up_w, down_w)
        pair_grad = backward_rows(scaled, gate_pre, up_pre, gate_w, up_w, down_w)
        weight_grad = jnp.dot(scaled.astype(jnp.float32).T, hidden.astype(jnp.float32))
        return expert_out, pair_grad, weight_grad

    out_all, grad_all, weight_all = lax.map(per_expert, jnp.arange(EXPERTS, dtype=jnp.int32))
    out_flat = out_all.reshape(EXPERTS * slab_rows, D)
    grad_flat = grad_all.reshape(EXPERTS * slab_rows, D)
    pair_index = flat_index.reshape(TOKENS, TOP)
    output = jnp.zeros((TOKENS, D), jnp.float32)
    token_grad = jnp.zeros((TOKENS, D), jnp.float32)
    for choice_index in range(TOP):
        rows_at = pair_index[:, choice_index]
        output = output + routing[:, choice_index][:, None] * out_flat[rows_at].astype(jnp.float32)
        token_grad = token_grad + grad_flat[rows_at].astype(jnp.float32)
    down_grad = weight_all / N_DP
    return output.astype(jnp.bfloat16), token_grad.astype(jnp.bfloat16), down_grad
```

```python
import jax
import jax.numpy as jnp
from jax import lax
from jax.experimental import pallas as pl
from jax.experimental.pallas import tpu as pltpu
from jax.sharding import Mesh
from jax.sharding import PartitionSpec as P

MESH = pl.DeviceIdType.MESH
F32 = jnp.float32
BF16 = jnp.bfloat16
SIDE = 8
BLOCKS = 16
CAP = 24
PAIR = 2 * CAP
ROWS = BLOCKS * CAP
WIDTH = 1024
FF = 384
SHARD = 16
ORDER = (8, 9, 10, 11, 4, 5, 6, 7, 12, 13, 14, 15, 2, 3, 1)


def mm(a, b):
    return jnp.dot(a, b, preferred_element_type=F32)


def mm_nt(a, b):
    return lax.dot_general(a, b, (((1,), (1,)), ((), ())), preferred_element_type=F32)


def mm_tn(a, b):
    return lax.dot_general(a, b, (((0,), (0,)), ((), ())), preferred_element_type=F32)


def kernel(
    tok_ref,
    ids_ref,
    rout_ref,
    wg_ref,
    wu_ref,
    wd_ref,
    go_ref,
    out_ref,
    tg_ref,
    dg_ref,
    sh,
    wbuf,
    sendb,
    recv,
    xs,
    gs,
    outb,
    back,
    dwb,
    rs1,
    s1b,
    rs2,
    pz,
    pzr,
    gx,
    p_s,
    p_r,
    s1_s,
    s1_r,
    up_s,
    up_r,
    dn_s,
    dn_r,
    d_s,
    d_r,
    b_s,
    b_r,
    q_s,
    q_r,
    t_s,
    t_r,
    e_s,
    e_r,
):
    y, x = lax.axis_index("y"), lax.axis_index("x")
    z, c = lax.axis_index("z"), lax.axis_index("c")

    def wrap(v):
        return lax.rem(v + 2 * SIDE, SIDE)

    sign = 1 - 2 * c
    partner = {"z": wrap(z + 4)}
    mix = lax.rem(z // 4 + lax.rem(x, 2), 2)

    def steps(i, core):
        k, f = i // 4, (i // 2) % 2
        way = 1 - 2 * core
        dz = (0, 1, 2 * way, -1)[k]
        return dz, f * way, i % 2

    def target(i):
        dz, dx, m = steps(i, c)
        return {"x": wrap(x + dx), "z": wrap(z + dz), "c": lax.rem(c + m, 2)}

    def origin(i):
        m = i % 2
        core = lax.rem(c + m, 2)
        dz, dx, _ = steps(i, core)
        return {"x": wrap(x - dx), "z": wrap(z - dz), "c": core}

    def copy(src, dst, send, recv_sem, device):
        return pltpu.make_async_remote_copy(
            src_ref=src,
            dst_ref=dst,
            send_sem=send,
            recv_sem=recv_sem,
            device_id=device,
            device_id_type=MESH,
        )

    barrier = pltpu.get_barrier_semaphore()

    def greet(device):
        pl.semaphore_signal(barrier, inc=1, device_id=device, device_id_type=MESH)

    for i in range(1, BLOCKS):
        greet(target(i))
        greet(origin(i))
    for o in range(1, SIDE):
        greet({"x": wrap(x + o)})
        greet({"y": wrap(y + o)})
    greet(partner)
    sh[0, 0] = wg_ref[0]
    sh[0, 1] = wu_ref[0]
    sh[0, 2] = wd_ref[0]

    ids = ids_ref[...]
    id0, id1 = ids[:, 0:1], ids[:, 1:2]
    n_tok = ids.shape[0]
    lanes = lax.broadcasted_iota(jnp.int32, (n_tok, 128), 1)
    named = jnp.where((lanes == id0) | (lanes == id1), 1.0, 0.0).astype(BF16)
    row_i = lax.broadcasted_iota(jnp.int32, (n_tok, n_tok), 0)
    col_i = lax.broadcasted_iota(jnp.int32, (n_tok, n_tok), 1)
    lower = jnp.where(col_i < row_i, 1.0, 0.0).astype(BF16)
    before = mm(lower, named)

    def slot_of(expert):
        rank = jnp.sum(jnp.where(lanes == expert, before, 0.0), axis=1, keepdims=True)
        k = ((expert >> 1) - z + SIDE) & 3
        f = ((expert >> 3) + x) & 1
        m = (expert + c) & 1
        return (k * 4 + f * 2 + m) * PAIR + rank.astype(jnp.int32)

    slot0, slot1 = slot_of(id0), slot_of(id1)
    slots = lax.broadcasted_iota(jnp.int32, (n_tok, BLOCKS * PAIR), 1)

    def mark(slot):
        return jnp.where(slots == slot, 1.0, 0.0)

    gx[0] = mark(slot0).astype(BF16)
    gx[1] = mark(slot1).astype(BF16)
    gx[2] = mark(slot0 + CAP).astype(BF16)
    gx[3] = mark(slot1 + CAP).astype(BF16)
    rout = rout_ref[...]
    r0, r1 = rout[:, 0:1], rout[:, 1:2]
    cot = go_ref[...].astype(F32)
    staged = jnp.concatenate(
        [tok_ref[...], (r0 * cot).astype(BF16), (r1 * cot).astype(BF16)], axis=0
    )

    pl.semaphore_wait(barrier, 2 * (BLOCKS - 1) + 2 * (SIDE - 1) + 1)

    swap = copy(sh.at[0], sh.at[1], p_s, p_r, partner)
    swap.start()

    def row_copy(which, i):
        off = 2 * i + (mix if which == 0 else 1 - mix)
        dest = {"x": lax.rem(x + off, SIDE)}
        return off, copy(
            sh.at[which], wbuf.at[y, x], s1_s.at[off], s1_r.at[off], dest
        )

    def row_sends(which):
        for i in range(4):
            off, sent = row_copy(which, i)
            if i == 0:

                @pl.when(off == 0)
                def _():
                    wbuf[y, x] = sh[which]

                @pl.when(off != 0)
                def _():
                    sent.start()
            else:
                sent.start()

    row_sends(0)

    chosen = jnp.concatenate([gx[0] + gx[1], gx[2], gx[3]], axis=0)
    quarter = BLOCKS * PAIR // 4
    for part in (2, 1, 3, 0):
        cols = chosen[:, part * quarter : (part + 1) * quarter]
        packed = mm_tn(cols, staged).astype(BF16)
        sendb[pl.ds(part * quarter, quarter)] = packed
        for i in ORDER:
            if i // 4 == part:
                here = pl.ds(i * PAIR, PAIR)
                copy(
                    sendb.at[here], recv.at[here], d_s.at[i], d_r.at[i], target(i)
                ).start()
    recv[pl.ds(0, PAIR)] = sendb[pl.ds(0, PAIR)]

    swap.wait_recv()
    row_sends(1)

    above, below = {"y": wrap(y + 1)}, {"y": wrap(y - 1)}

    def place(p):
        return lax.rem(x - p + SIDE, SIDE)

    def up_copy(d, p):
        block = wbuf.at[wrap(y - d), place(p)]
        return copy(block, block, up_s.at[d, p], up_r.at[d, p], above)

    def down_copy(d, p):
        block = wbuf.at[wrap(y + d), place(p)]
        return copy(block, block, dn_s.at[d, p], dn_r.at[d, p], below)

    def up_arrived(d, p):
        block = wbuf.at[wrap(y - d - 1), place(p)]
        copy(block, block, up_s.at[d, p], up_r.at[d, p], above).wait_recv()

    def down_arrived(d, p):
        block = wbuf.at[wrap(y + d + 1), place(p)]
        copy(block, block, dn_s.at[d, p], dn_r.at[d, p], below).wait_recv()

    def first(p, carry):
        @pl.when(p != 0)
        def _():
            block = wbuf.at[y, place(p)]
            copy(block, block, s1_s.at[p], s1_r.at[p], above).wait_recv()

        up_copy(0, p).start()
        down_copy(0, p).start()
        return carry

    lax.fori_loop(0, SIDE, first, 0)

    for d in (1, 2):

        def onward(p, carry, d=d):
            up_arrived(d - 1, p)
            up_copy(d, p).start()
            down_arrived(d - 1, p)
            down_copy(d, p).start()
            return carry

        lax.fori_loop(0, SIDE, onward, 0)

    half = SIDE // 2

    def last(p, carry):
        up_arrived(2, p)
        up_copy(3, p).start()
        down_arrived(2, p)
        up_arrived(2, p + half)
        down_arrived(2, p + half)
        down_copy(3, p + half).start()
        return carry

    lax.fori_loop(0, half, last, 0)

    for i in ORDER:
        here = pl.ds(i * PAIR, PAIR)
        copy(sendb.at[here], recv.at[here], d_s.at[i], d_r.at[i], target(i)).wait_recv()
    for i in range(0, BLOCKS, 2):
        both = recv[pl.ds(i * PAIR, 2 * PAIR)].astype(F32)
        here = pl.ds(i * CAP, 2 * CAP)
        xs[here] = jnp.concatenate(
            [both[0:CAP], both[PAIR : PAIR + CAP]], axis=0
        ).astype(BF16)
        gs[here] = jnp.concatenate(
            [both[CAP:PAIR], both[PAIR + CAP : 2 * PAIR]], axis=0
        ).astype(BF16)

    def final(p, carry):
        up_arrived(3, p)
        down_arrived(3, p + half)
        return carry

    lax.fori_loop(0, half, final, 0)

    def weight(which):
        return wbuf[:, :, which].reshape(WIDTH, FF)

    gate_w, up_w, down_w = weight(0), weight(1), weight(2)
    x_rows, g_rows = xs[...], gs[...]
    gate = mm(x_rows, gate_w)
    up = mm(x_rows, up_w)
    sig = jax.nn.sigmoid(gate)
    act = gate * sig
    hidden = (act * up).astype(BF16)
    dw = mm_tn(g_rows, hidden)
    dwb[...] = dw.astype(BF16).reshape(SIDE, SIDE * SHARD, FF)

    def sum_copy(o):
        to = wrap(y + o)
        return copy(dwb.at[to], rs1.at[o], q_s.at[o], q_r.at[o], {"y": to})

    for o in (4, 3, 5, 2, 6, 1, 7):
        sum_copy(o).start()
    hid_grad = mm(g_rows, down_w)
    gate_grad = (hid_grad * up * (sig * (1.0 + gate * (1.0 - sig)))).astype(BF16)
    up_grad = (hid_grad * act).astype(BF16)

    def result_copy(i):
        here = pl.ds(i * PAIR, PAIR)
        return copy(outb.at[here], back.at[here], b_s.at[i], b_r.at[i], origin(i))

    part_rows = 4 * CAP
    for part in (2, 1, 3, 0):
        rows = slice(part * part_rows, (part + 1) * part_rows)
        made = mm_nt(hidden[rows], down_w)
        grad = mm_nt(gate_grad[rows], gate_w) + mm_nt(up_grad[rows], up_w)
        pieces = []
        for j in range(4):
            pieces.append(made[j * CAP : (j + 1) * CAP])
            pieces.append(grad[j * CAP : (j + 1) * CAP])
        outb[pl.ds(part * 4 * PAIR, 4 * PAIR)] = jnp.concatenate(pieces, axis=0).astype(
            BF16
        )
        for i in ORDER:
            if i // 4 == part:
                result_copy(i).start()
    back[pl.ds(0, PAIR)] = outb[pl.ds(0, PAIR)]

    total = dwb[y].astype(F32)
    for o in (1, 7, 2, 6, 3, 5, 4):
        sum_copy(o).wait_recv()
        total = total + rs1[o].astype(F32)
    s1b[...] = total.astype(BF16).reshape(SIDE, SHARD, FF)

    def row_sum_copy(o):
        to = wrap(x + o)
        return copy(s1b.at[to], rs2.at[o], t_s.at[o], t_r.at[o], {"x": to})

    for o in (4, 3, 5, 2, 6, 1, 7):
        row_sum_copy(o).start()
    same, other = s1b[x].astype(F32), None
    for o in range(1, SIDE):
        row_sum_copy(o).wait_recv()
        term = rs2[o].astype(F32)
        if o % 2 == 0:
            same = same + term
        else:
            other = term if other is None else other + term
    pz[0] = same
    pz[1] = other
    trade = copy(pz.at[1 - mix], pzr, e_s, e_r, partner)
    trade.start()

    for i in ORDER:
        result_copy(i).wait_recv()
    rows_back = back[...]
    out0, out1 = mm(gx[0], rows_back), mm(gx[1], rows_back)
    out_ref[...] = (r0 * out0 + r1 * out1).astype(BF16)
    tg_ref[...] = mm(gx[2] + gx[3], rows_back).astype(BF16)

    trade.wait_recv()
    dg_ref[0] = (pz[mix] + pzr[...]) * (1.0 / (SIDE * SIDE))

    swap.wait_send()
    trade.wait_send()
    for which in (0, 1):
        for i in range(4):
            off, sent = row_copy(which, i)
            if i == 0:

                @pl.when(off != 0)
                def _():
                    sent.wait_send()
            else:
                sent.wait_send()
    for d in (0, 1, 2):

        def drained(p, carry, d=d):
            up_copy(d, p).wait_send()
            down_copy(d, p).wait_send()
            return carry

        lax.fori_loop(0, SIDE, drained, 0)

    def drained_last(p, carry):
        up_copy(3, p).wait_send()
        down_copy(3, p + half).wait_send()
        return carry

    lax.fori_loop(0, half, drained_last, 0)
    for i in ORDER:
        here = pl.ds(i * PAIR, PAIR)
        copy(sendb.at[here], recv.at[here], d_s.at[i], d_r.at[i], target(i)).wait_send()
        result_copy(i).wait_send()
    for o in range(1, SIDE):
        sum_copy(o).wait_send()
        row_sum_copy(o).wait_send()


def local(tokens, expert_ids, routing, w_gate, w_up, w_down, grad_out):
    n_tok = tokens.shape[0]
    vmem = pl.BlockSpec(memory_space=pltpu.VMEM)
    dma = pltpu.SemaphoreType.DMA
    return pl.pallas_call(
        kernel,
        out_shape=(
            jax.ShapeDtypeStruct((n_tok, WIDTH), BF16),
            jax.ShapeDtypeStruct((n_tok, WIDTH), BF16),
            jax.ShapeDtypeStruct((1, SHARD, FF), F32),
        ),
        in_specs=[vmem] * 7,
        out_specs=(vmem, vmem, vmem),
        scratch_shapes=[
            pltpu.VMEM((2, 3, SHARD, FF), BF16),
            pltpu.VMEM((SIDE, SIDE, 3, SHARD, FF), BF16),
            pltpu.VMEM((BLOCKS * PAIR, WIDTH), BF16),
            pltpu.VMEM((BLOCKS * PAIR, WIDTH), BF16),
            pltpu.VMEM((ROWS, WIDTH), BF16),
            pltpu.VMEM((ROWS, WIDTH), BF16),
            pltpu.VMEM((BLOCKS * PAIR, WIDTH), BF16),
            pltpu.VMEM((BLOCKS * PAIR, WIDTH), BF16),
            pltpu.VMEM((SIDE, SIDE * SHARD, FF), BF16),
            pltpu.VMEM((SIDE, SIDE * SHARD, FF), BF16),
            pltpu.VMEM((SIDE, SHARD, FF), BF16),
            pltpu.VMEM((SIDE, SHARD, FF), BF16),
            pltpu.VMEM((2, SHARD, FF), F32),
            pltpu.VMEM((SHARD, FF), F32),
            pltpu.VMEM((4, n_tok, BLOCKS * PAIR), BF16),
            dma,
            dma,
            dma((SIDE,)),
            dma((SIDE,)),
            dma((4, SIDE)),
            dma((4, SIDE)),
            dma((4, SIDE)),
            dma((4, SIDE)),
            dma((BLOCKS,)),
            dma((BLOCKS,)),
            dma((BLOCKS,)),
            dma((BLOCKS,)),
            dma((SIDE,)),
            dma((SIDE,)),
            dma((SIDE,)),
            dma((SIDE,)),
            dma,
            dma,
        ],
        compiler_params=pltpu.CompilerParams(
            collective_id=0,
            has_side_effects=True,
            vmem_limit_bytes=48 * 1024 * 1024,
        ),
        cost_estimate=pl.CostEstimate(
            flops=3_000_000_000, bytes_accessed=2_000_000, transcendentals=150_000
        ),
    )(tokens, expert_ids, routing, w_gate, w_up, w_down, grad_out)


def solution(mesh):
    finer = Mesh(mesh.devices.reshape(SIDE, SIDE, SIDE, 2), ("y", "x", "z", "c"))
    every = ("y", "x", "z", "c")
    rows = P(every, None)
    weights = P(("z", "c"), ("y", "x"), None)
    return jax.shard_map(
        local,
        mesh=finer,
        in_specs=(rows, rows, rows, weights, weights, weights, rows),
        out_specs=(rows, rows, weights),
        check_vma=False,
    )
```

```python
import jax
import jax.numpy as jnp
from jax import lax
from jax.experimental import pallas as pl
from jax.experimental.pallas import tpu as pltpu
from jax.sharding import Mesh
from jax.sharding import PartitionSpec as P

MESH = pl.DeviceIdType.MESH
F32 = jnp.float32
BF16 = jnp.bfloat16
SIDE = 8
BLOCKS = 16
CAP = 24
PAIR = 2 * CAP
ROWS = BLOCKS * CAP
WIDTH = 1024
FF = 384
SHARD = 16
WIDE = 256
ORDER = (8, 9, 10, 11, 4, 5, 6, 7, 12, 13, 14, 15, 2, 3, 1)


def mm(a, b):
    return jnp.dot(a, b, preferred_element_type=F32)


def mm_nt(a, b):
    return lax.dot_general(a, b, (((1,), (1,)), ((), ())), preferred_element_type=F32)


def mm_tn(a, b):
    return lax.dot_general(a, b, (((0,), (0,)), ((), ())), preferred_element_type=F32)


def kernel(
    tok_any,
    ids_any,
    rout_any,
    wg_any,
    wu_any,
    wd_any,
    go_any,
    out_ref,
    tg_ref,
    dg_ref,
    tok,
    cot_in,
    ids_v,
    rout_v,
    sh,
    wbuf,
    sendb,
    recv,
    xs,
    gs,
    gst,
    acc,
    outb,
    back,
    dwy,
    ry1,
    sy1,
    ry2,
    dwx,
    rx1,
    sx1,
    rx2,
    back_mark,
    in_s,
    p_s,
    p_r,
    s1_s,
    s1_r,
    up_s,
    up_r,
    dn_s,
    dn_r,
    d_s,
    d_r,
    b_s,
    b_r,
    y1_s,
    y1_r,
    y2_s,
    y2_r,
    x1_s,
    x1_r,
    x2_s,
    x2_r,
):
    y, x = lax.axis_index("y"), lax.axis_index("x")
    z, c = lax.axis_index("z"), lax.axis_index("c")

    def wrap(v):
        return lax.rem(v + 2 * SIDE, SIDE)

    far = wrap(z + 4)
    partner = {"z": far}
    mix = lax.rem(z // 4 + lax.rem(x, 2), 2)

    def steps(i, core):
        k, f = i // 4, (i // 2) % 2
        way = 1 - 2 * core
        dz = (0, 1, 2 * way, -1)[k]
        return dz, f * way, i % 2

    def target(i):
        dz, dx, m = steps(i, c)
        return {"x": wrap(x + dx), "z": wrap(z + dz), "c": lax.rem(c + m, 2)}

    def origin(i):
        m = i % 2
        core = lax.rem(c + m, 2)
        dz, dx, _ = steps(i, core)
        return {"x": wrap(x - dx), "z": wrap(z - dz), "c": core}

    def copy(src, dst, send, recv_sem, device):
        return pltpu.make_async_remote_copy(
            src_ref=src,
            dst_ref=dst,
            send_sem=send,
            recv_sem=recv_sem,
            device_id=device,
            device_id_type=MESH,
        )

    barrier = pltpu.get_barrier_semaphore()

    def greet(device):
        pl.semaphore_signal(barrier, inc=1, device_id=device, device_id_type=MESH)

    loads = []
    for n, (src, dst) in enumerate(
        (
            (wg_any.at[0], sh.at[0, 0]),
            (wu_any.at[0], sh.at[0, 1]),
            (wd_any.at[0], sh.at[0, 2]),
            (ids_any, ids_v),
            (rout_any, rout_v),
            (tok_any, tok),
            (go_any, cot_in),
        )
    ):
        load = pltpu.make_async_copy(src, dst, in_s.at[n])
        load.start()
        loads.append(load)

    greet(partner)
    for o in range(1, SIDE):
        greet({"x": wrap(x + o)})
        greet({"y": wrap(y + o)})
        greet({"x": wrap(x + o), "z": far})
        greet({"y": wrap(y + o), "z": far})
    for i in range(1, BLOCKS):
        greet(target(i))
        greet(origin(i))
    for load in loads[:3]:
        load.wait()
    pl.semaphore_wait(barrier, 2 * (BLOCKS - 1) + 4 * (SIDE - 1) + 1)

    swap = copy(sh.at[0], sh.at[1], p_s, p_r, partner)
    swap.start()

    def row_copy(which, i):
        off = 2 * i + (mix if which == 0 else 1 - mix)
        dest = {"x": lax.rem(x + off, SIDE)}
        return off, copy(
            sh.at[which], wbuf.at[y, x], s1_s.at[off], s1_r.at[off], dest
        )

    def row_sends(which):
        for i in range(4):
            off, sent = row_copy(which, i)
            if i == 0:

                @pl.when(off == 0)
                def _():
                    wbuf[y, x] = sh[which]

                @pl.when(off != 0)
                def _():
                    sent.start()
            else:
                sent.start()

    row_sends(0)

    above, below = {"y": wrap(y + 1)}, {"y": wrap(y - 1)}

    def away(j):
        odd = lax.rem(j, 2)
        return odd * ((j + 1) // 2) + (1 - odd) * lax.rem(SIDE - j // 2, SIDE)

    def place(j):
        return lax.rem(x - away(j) + SIDE, SIDE)

    def up_copy(d, j):
        block = wbuf.at[wrap(y - d), place(j)]
        return copy(block, block, up_s.at[d, j], up_r.at[d, j], above)

    def down_copy(d, j):
        block = wbuf.at[wrap(y + d), place(j)]
        return copy(block, block, dn_s.at[d, j], dn_r.at[d, j], below)

    def up_arrived(d, j):
        block = wbuf.at[wrap(y - d - 1), place(j)]
        copy(block, block, up_s.at[d, j], up_r.at[d, j], above).wait_recv()

    def down_arrived(d, j):
        block = wbuf.at[wrap(y + d + 1), place(j)]
        copy(block, block, dn_s.at[d, j], dn_r.at[d, j], below).wait_recv()

    @pl.when(mix == 0)
    def _():
        up_copy(0, 0).start()
        down_copy(0, 0).start()

    for load in loads[3:]:
        load.wait()
    id0, id1 = ids_v[0:1], ids_v[1:2]
    n_tok = id0.shape[1]
    names = lax.broadcasted_iota(jnp.int32, (16, n_tok), 0)
    named = jnp.where((names == id0) | (names == id1), 1.0, 0.0).astype(BF16)
    row_i = lax.broadcasted_iota(jnp.int32, (n_tok, n_tok), 0)
    col_i = lax.broadcasted_iota(jnp.int32, (n_tok, n_tok), 1)
    before = mm(named, jnp.where(row_i < col_i, 1.0, 0.0).astype(BF16))

    def slot_of(expert):
        rank = jnp.sum(jnp.where(names == expert, before, 0.0), axis=0, keepdims=True)
        k = ((expert >> 1) - z + SIDE) & 3
        f = ((expert >> 3) + x) & 1
        m = (expert + c) & 1
        return (k * 4 + f * 2 + m) * PAIR + rank.astype(jnp.int32)

    slot0, slot1 = slot_of(id0), slot_of(id1)

    def mark(first, count, slot):
        slots = lax.broadcasted_iota(jnp.int32, (count, n_tok), 0) + first
        return jnp.where(slots == slot, 1.0, 0.0)

    def column(row):
        return jnp.transpose(jnp.broadcast_to(row, (n_tok, n_tok)))[:, 0:1]

    r0, r1 = column(rout_v[0:1]), column(rout_v[1:2])
    cot = cot_in[...].astype(F32)
    staged = jnp.concatenate(
        [tok[...], (r0 * cot).astype(BF16), (r1 * cot).astype(BF16)], axis=0
    )

    quarter = BLOCKS * PAIR // 4

    def pack(part):
        first = part * quarter
        m0, m1 = mark(first, quarter, slot0), mark(first, quarter, slot1)
        g0 = mark(first, quarter, slot0 + CAP)
        g1 = mark(first, quarter, slot1 + CAP)
        chosen = jnp.concatenate(
            [(m0 + m1).astype(BF16), g0.astype(BF16), g1.astype(BF16)], axis=1
        )
        sendb[pl.ds(first, quarter)] = mm(chosen, staged).astype(BF16)
        for i in ORDER:
            if i // 4 == part:
                here = pl.ds(i * PAIR, PAIR)
                copy(
                    sendb.at[here], recv.at[here], d_s.at[i], d_r.at[i], target(i)
                ).start()

    pack(2)
    swap.wait_recv()
    row_sends(1)

    @pl.when(mix == 1)
    def _():
        up_copy(0, 0).start()
        down_copy(0, 0).start()

    pack(1)
    pack(3)
    pack(0)
    recv[pl.ds(0, PAIR)] = sendb[pl.ds(0, PAIR)]

    def first_step(j, carry):
        block = wbuf.at[y, place(j)]
        copy(block, block, s1_s.at[away(j)], s1_r.at[away(j)], above).wait_recv()
        up_copy(0, j).start()
        down_copy(0, j).start()
        return carry

    lax.fori_loop(1, SIDE, first_step, 0)

    for d in (1, 2):

        def onward(p, carry, d=d):
            up_arrived(d - 1, p)
            up_copy(d, p).start()
            down_arrived(d - 1, p)
            down_copy(d, p).start()
            return carry

        lax.fori_loop(0, SIDE, onward, 0)

    half = SIDE // 2

    def last(p, carry):
        up_arrived(2, p)
        up_copy(3, p).start()
        down_arrived(2, p)
        up_arrived(2, p + half)
        down_arrived(2, p + half)
        down_copy(3, p + half).start()
        return carry

    lax.fori_loop(0, half, last, 0)

    for i in ORDER:
        here = pl.ds(i * PAIR, PAIR)
        copy(sendb.at[here], recv.at[here], d_s.at[i], d_r.at[i], target(i)).wait_recv()
    for i in range(0, BLOCKS, 2):
        both = recv[pl.ds(i * PAIR, 2 * PAIR)].astype(F32)
        here = pl.ds(i * CAP, 2 * CAP)
        xs[here] = jnp.concatenate(
            [both[0:CAP], both[PAIR : PAIR + CAP]], axis=0
        ).astype(BF16)
        gs[here] = jnp.concatenate(
            [both[CAP:PAIR], both[PAIR + CAP : 2 * PAIR]], axis=0
        ).astype(BF16)

    depth = SIDE * SHARD

    def accumulate(shifts, start):
        blocks = [wrap(y + s) for s in shifts]
        cols = [pl.ds(pl.multiple_of(b * depth, depth), depth) for b in blocks]
        x_part = jnp.concatenate([xs[:, at] for at in cols], axis=1)
        g_part = jnp.concatenate([gs[:, at] for at in cols], axis=1)
        for which, rows in ((0, x_part), (1, x_part), (2, g_part)):
            held = jnp.concatenate(
                [wbuf[b, :, which].reshape(depth, FF) for b in blocks], axis=0
            )
            term = mm(rows, held)
            acc[which] = term if start else acc[which] + term

    accumulate((0, 1), True)
    accumulate((-1, 2), False)
    accumulate((-2, 3), False)
    accumulate((-3,), False)
    gst[...] = jnp.transpose(gs[...])
    for k in range(3):
        whole = (
            mark(0, BLOCKS * PAIR, slot0)
            if k == 0
            else mark(0, BLOCKS * PAIR, slot1)
            if k == 1
            else mark(0, BLOCKS * PAIR, slot0 + CAP)
            + mark(0, BLOCKS * PAIR, slot1 + CAP)
        )
        back_mark[pl.ds(k * n_tok, n_tok)] = jnp.transpose(whole).astype(BF16)

    def final(p, carry):
        up_arrived(3, p)
        down_arrived(3, p + half)
        return carry

    lax.fori_loop(0, half, final, 0)
    accumulate((4,), False)

    def weight(which):
        return wbuf[:, :, which].reshape(WIDTH, FF)

    gate_w, up_w, down_w = weight(0), weight(1), weight(2)
    gate, up = acc[0], acc[1]
    sig = jax.nn.sigmoid(gate)
    act = gate * sig
    hidden = (act * up).astype(BF16)

    dw = mm(gst[...], hidden).astype(BF16)
    dwy[...] = dw[:, 0:WIDE].reshape(SIDE, SIDE * SHARD, WIDE)
    dwx[...] = dw[:, WIDE:FF].reshape(SIDE, SIDE, SHARD, FF - WIDE)

    def y1_copy(o):
        to = wrap(y + o)
        return copy(dwy.at[to], ry1.at[o], y1_s.at[o], y1_r.at[o], {"y": to})

    def x1_copy(o):
        to = wrap(x + o)
        return copy(dwx.at[:, to], rx1.at[o], x1_s.at[o], x1_r.at[o], {"x": to})

    for o in (4, 3, 5, 2, 6, 1, 7):
        y1_copy(o).start()
        x1_copy(o).start()
    hid_grad = acc[2]
    gate_grad = (hid_grad * up * (sig * (1.0 + gate * (1.0 - sig)))).astype(BF16)
    up_grad = (hid_grad * act).astype(BF16)

    def result_copy(i):
        here = pl.ds(i * PAIR, PAIR)
        return copy(outb.at[here], back.at[here], b_s.at[i], b_r.at[i], origin(i))

    part_rows = 4 * CAP
    for part in (2, 1, 3, 0):
        rows = slice(part * part_rows, (part + 1) * part_rows)
        made = mm_nt(hidden[rows], down_w)
        grad = mm_nt(gate_grad[rows], gate_w) + mm_nt(up_grad[rows], up_w)
        pieces = []
        for j in range(4):
            pieces.append(made[j * CAP : (j + 1) * CAP])
            pieces.append(grad[j * CAP : (j + 1) * CAP])
        outb[pl.ds(part * 4 * PAIR, 4 * PAIR)] = jnp.concatenate(pieces, axis=0).astype(
            BF16
        )
        for i in ORDER:
            if i // 4 == part:
                result_copy(i).start()
    back[pl.ds(0, PAIR)] = outb[pl.ds(0, PAIR)]

    total = dwy[y].astype(F32)
    for o in (1, 7, 2, 6, 3, 5, 4):
        y1_copy(o).wait_recv()
        total = total + ry1[o].astype(F32)
    sy1[...] = total.astype(BF16).reshape(SIDE, SHARD, WIDE)

    own_plane = wrap(z + 4 * mix)

    def y2_copy(o):
        to = wrap(x + o)
        slot = 2 * (o // 2) + mix
        return copy(
            sy1.at[to],
            ry2.at[slot],
            y2_s.at[o],
            y2_r.at[slot],
            {"x": to, "z": own_plane},
        )

    y2_copy_self = y2_copy(0)

    @pl.when(mix == 0)
    def _():
        ry2[0] = sy1[x]

    @pl.when(mix == 1)
    def _():
        y2_copy_self.start()

    for o in (4, 3, 5, 2, 6, 1, 7):
        y2_copy(o).start()

    same = dwx[:, x].astype(F32)
    other = None
    for o in (1, 7, 2, 6, 3, 5, 4):
        x1_copy(o).wait_recv()
        term = rx1[o].astype(F32)
        if o % 2 == 0:
            same = same + term
        else:
            other = term if other is None else other + term
    sx1[0] = same.astype(BF16)
    sx1[1] = other.astype(BF16)

    def x2_copy(which, o):
        to = wrap(y + o)
        held = lax.rem(mix + which, 2)
        return copy(
            sx1.at[held, to],
            rx2.at[which, o],
            x2_s.at[which, o],
            x2_r.at[which, o],
            {"y": to, "z": wrap(z + 4 * which)},
        )

    rx2[0, 0] = sx1[mix, y]
    x2_copy(1, 0).start()
    for o in (4, 3, 5, 2, 6, 1, 7):
        x2_copy(0, o).start()
        x2_copy(1, o).start()

    for i in ORDER:
        result_copy(i).wait_recv()
    from_mark = mm(back_mark[...], back[...])
    out_ref[...] = (r0 * from_mark[0:n_tok] + r1 * from_mark[n_tok : 2 * n_tok]).astype(
        BF16
    )
    tg_ref[...] = from_mark[2 * n_tok : 3 * n_tok].astype(BF16)

    def y2_arrived(slot):
        copy(
            sy1.at[0], ry2.at[slot], y2_s.at[0], y2_r.at[slot], {"z": own_plane}
        ).wait_recv()

    @pl.when(mix == 1)
    def _():
        y2_arrived(0)

    for slot in range(1, SIDE):
        y2_arrived(slot)
    for o in range(SIDE):
        for which in (0, 1):
            if o or which:
                x2_copy(which, o).wait_recv()
    scale = 1.0 / (SIDE * SIDE)
    wide = ry2[0].astype(F32)
    for slot in range(1, SIDE):
        wide = wide + ry2[slot].astype(F32)
    narrow = None
    for o in range(SIDE):
        for which in (0, 1):
            term = rx2[which, o].astype(F32)
            narrow = term if narrow is None else narrow + term
    dg_ref[0] = jnp.concatenate([wide, narrow], axis=1) * scale

    swap.wait_send()
    for which in (0, 1):
        for i in range(4):
            off, sent = row_copy(which, i)
            if i == 0:

                @pl.when(off != 0)
                def _():
                    sent.wait_send()
            else:
                sent.wait_send()
    for d in (0, 1, 2):

        def drained(p, carry, d=d):
            up_copy(d, p).wait_send()
            down_copy(d, p).wait_send()
            return carry

        lax.fori_loop(0, SIDE, drained, 0)

    def drained_last(p, carry):
        up_copy(3, p).wait_send()
        down_copy(3, p + half).wait_send()
        return carry

    lax.fori_loop(0, half, drained_last, 0)
    for i in ORDER:
        here = pl.ds(i * PAIR, PAIR)
        copy(sendb.at[here], recv.at[here], d_s.at[i], d_r.at[i], target(i)).wait_send()
        result_copy(i).wait_send()

    @pl.when(mix == 1)
    def _():
        y2_copy_self.wait_send()

    x2_copy(1, 0).wait_send()
    for o in range(1, SIDE):
        y1_copy(o).wait_send()
        x1_copy(o).wait_send()
        y2_copy(o).wait_send()
        x2_copy(0, o).wait_send()
        x2_copy(1, o).wait_send()


def local(tokens, expert_ids, routing, w_gate, w_up, w_down, grad_out):
    n_tok = tokens.shape[0]
    vmem = pl.BlockSpec(memory_space=pltpu.VMEM)
    hbm = pl.BlockSpec(memory_space=pltpu.HBM)
    dma = pltpu.SemaphoreType.DMA
    narrow = FF - WIDE
    return pl.pallas_call(
        kernel,
        out_shape=(
            jax.ShapeDtypeStruct((n_tok, WIDTH), BF16),
            jax.ShapeDtypeStruct((n_tok, WIDTH), BF16),
            jax.ShapeDtypeStruct((1, SHARD, FF), F32),
        ),
        in_specs=[hbm] * 7,
        out_specs=(vmem, vmem, vmem),
        scratch_shapes=[
            pltpu.VMEM((n_tok, WIDTH), BF16),
            pltpu.VMEM((n_tok, WIDTH), BF16),
            pltpu.VMEM((2, n_tok), jnp.int32),
            pltpu.VMEM((2, n_tok), F32),
            pltpu.VMEM((2, 3, SHARD, FF), BF16),
            pltpu.VMEM((SIDE, SIDE, 3, SHARD, FF), BF16),
            pltpu.VMEM((BLOCKS * PAIR, WIDTH), BF16),
            pltpu.VMEM((BLOCKS * PAIR, WIDTH), BF16),
            pltpu.VMEM((ROWS, WIDTH), BF16),
            pltpu.VMEM((ROWS, WIDTH), BF16),
            pltpu.VMEM((WIDTH, ROWS), BF16),
            pltpu.VMEM((3, ROWS, FF), F32),
            pltpu.VMEM((BLOCKS * PAIR, WIDTH), BF16),
            pltpu.VMEM((BLOCKS * PAIR, WIDTH), BF16),
            pltpu.VMEM((SIDE, SIDE * SHARD, WIDE), BF16),
            pltpu.VMEM((SIDE, SIDE * SHARD, WIDE), BF16),
            pltpu.VMEM((SIDE, SHARD, WIDE), BF16),
            pltpu.VMEM((SIDE, SHARD, WIDE), BF16),
            pltpu.VMEM((SIDE, SIDE, SHARD, narrow), BF16),
            pltpu.VMEM((SIDE, SIDE, SHARD, narrow), BF16),
            pltpu.VMEM((2, SIDE, SHARD, narrow), BF16),
            pltpu.VMEM((2, SIDE, SHARD, narrow), BF16),
            pltpu.VMEM((3 * n_tok, BLOCKS * PAIR), BF16),
            dma((7,)),
            dma,
            dma,
            dma((SIDE,)),
            dma((SIDE,)),
            dma((4, SIDE)),
            dma((4, SIDE)),
            dma((4, SIDE)),
            dma((4, SIDE)),
            dma((BLOCKS,)),
            dma((BLOCKS,)),
            dma((BLOCKS,)),
            dma((BLOCKS,)),
            dma((SIDE,)),
            dma((SIDE,)),
            dma((SIDE,)),
            dma((SIDE,)),
            dma((SIDE,)),
            dma((SIDE,)),
            dma((2, SIDE)),
            dma((2, SIDE)),
        ],
        compiler_params=pltpu.CompilerParams(
            collective_id=0,
            has_side_effects=True,
            vmem_limit_bytes=56 * 1024 * 1024,
        ),
        cost_estimate=pl.CostEstimate(
            flops=3_000_000_000, bytes_accessed=2_000_000, transcendentals=150_000
        ),
    )(tokens, expert_ids.T, routing.T, w_gate, w_up, w_down, grad_out)


def solution(mesh):
    finer = Mesh(mesh.devices.reshape(SIDE, SIDE, SIDE, 2), ("y", "x", "z", "c"))
    every = ("y", "x", "z", "c")
    rows = P(every, None)
    weights = P(("z", "c"), ("y", "x"), None)
    return jax.shard_map(
        local,
        mesh=finer,
        in_specs=(rows, rows, rows, weights, weights, weights, rows),
        out_specs=(rows, rows, weights),
        check_vma=False,
    )
```

```python
import jax
import jax.numpy as jnp
from jax import lax
from jax.experimental import pallas as pl
from jax.experimental.pallas import tpu as pltpu
from jax.sharding import Mesh
from jax.sharding import PartitionSpec as P

MESH = pl.DeviceIdType.MESH
F32 = jnp.float32
BF16 = jnp.bfloat16
SIDE = 8
BLOCKS = 16
CAP = 24
PAIR = 2 * CAP
ROWS = BLOCKS * CAP
WIDTH = 1024
FF = 384
SHARD = 16
WIDE = 256
ORDER = (8, 9, 10, 11, 4, 5, 6, 7, 12, 13, 14, 15, 2, 3, 1)


def mm(a, b):
    return jnp.dot(a, b, preferred_element_type=F32)


def mm_nt(a, b):
    return lax.dot_general(a, b, (((1,), (1,)), ((), ())), preferred_element_type=F32)


def mm_tn(a, b):
    return lax.dot_general(a, b, (((0,), (0,)), ((), ())), preferred_element_type=F32)


def kernel(
    tok_any,
    ids_any,
    rout_any,
    wg_any,
    wu_any,
    wd_any,
    go_any,
    out_ref,
    tg_ref,
    dg_ref,
    tok,
    cot_in,
    ids_v,
    rout_v,
    sh,
    wbuf,
    sendb,
    recv,
    xs,
    gs,
    gst,
    acc,
    outb,
    back,
    dwy,
    ry1,
    sy1,
    ry2,
    dwx,
    rx1,
    sx1,
    rx2,
    back_mark,
    in_s,
    p_s,
    p_r,
    s1_s,
    s1_r,
    up_s,
    up_r,
    dn_s,
    dn_r,
    d_s,
    d_r,
    b_s,
    b_r,
    y1_s,
    y1_r,
    y2_s,
    y2_r,
    x1_s,
    x1_r,
    x2_s,
    x2_r,
):
    y, x = lax.axis_index("y"), lax.axis_index("x")
    z, c = lax.axis_index("z"), lax.axis_index("c")

    def wrap(v):
        return lax.rem(v + 2 * SIDE, SIDE)

    far = wrap(z + 4)
    partner = {"z": far}
    mix = lax.rem(z // 4 + lax.rem(x, 2), 2)

    def steps(i, core):
        k, f = i // 4, (i // 2) % 2
        way = 1 - 2 * core
        dz = (0, 1, 2 * way, -1)[k]
        return dz, f * way, i % 2

    def target(i):
        dz, dx, m = steps(i, c)
        return {"x": wrap(x + dx), "z": wrap(z + dz), "c": lax.rem(c + m, 2)}

    def origin(i):
        m = i % 2
        core = lax.rem(c + m, 2)
        dz, dx, _ = steps(i, core)
        return {"x": wrap(x - dx), "z": wrap(z - dz), "c": core}

    def copy(src, dst, send, recv_sem, device):
        return pltpu.make_async_remote_copy(
            src_ref=src,
            dst_ref=dst,
            send_sem=send,
            recv_sem=recv_sem,
            device_id=device,
            device_id_type=MESH,
        )

    barrier = pltpu.get_barrier_semaphore()

    def greet(device):
        pl.semaphore_signal(barrier, inc=1, device_id=device, device_id_type=MESH)

    loads = []
    for n, (src, dst) in enumerate(
        (
            (wg_any.at[0], sh.at[0, 0]),
            (wu_any.at[0], sh.at[0, 1]),
            (wd_any.at[0], sh.at[0, 2]),
            (ids_any, ids_v),
            (rout_any, rout_v),
            (tok_any, tok),
            (go_any, cot_in),
        )
    ):
        load = pltpu.make_async_copy(src, dst, in_s.at[n])
        load.start()
        loads.append(load)

    greet(partner)
    for o in range(1, SIDE):
        greet({"x": wrap(x + o)})
        greet({"y": wrap(y + o)})
        greet({"x": wrap(x + o), "z": far})
        greet({"y": wrap(y + o), "z": far})
    for i in range(1, BLOCKS):
        greet(target(i))
        greet(origin(i))
    for load in loads[:3]:
        load.wait()
    pl.semaphore_wait(barrier, 2 * (BLOCKS - 1) + 4 * (SIDE - 1) + 1)

    swap = copy(sh.at[0], sh.at[1], p_s, p_r, partner)
    swap.start()

    def row_copy(which, i):
        off = 2 * i + (mix if which == 0 else 1 - mix)
        dest = {"x": lax.rem(x + off, SIDE)}
        return off, copy(
            sh.at[which], wbuf.at[y, x], s1_s.at[off], s1_r.at[off], dest
        )

    def row_sends(which):
        for i in range(4):
            off, sent = row_copy(which, i)
            if i == 0:

                @pl.when(off == 0)
                def _():
                    wbuf[y, x] = sh[which]

                @pl.when(off != 0)
                def _():
                    sent.start()
            else:
                sent.start()

    row_sends(0)

    above, below = {"y": wrap(y + 1)}, {"y": wrap(y - 1)}

    def away(j):
        odd = lax.rem(j, 2)
        return odd * ((j + 1) // 2) + (1 - odd) * lax.rem(SIDE - j // 2, SIDE)

    def place(j):
        return lax.rem(x - away(j) + SIDE, SIDE)

    def ring_block(row, j, part):
        return wbuf.at[wrap(row), place(j), pl.ds(2 * part, 2 - part)]

    def up_copy(part, d, j):
        block = ring_block(y - d, j, part)
        return copy(block, block, up_s.at[part, d, j], up_r.at[part, d, j], above)

    def down_copy(part, d, j):
        block = ring_block(y + d, j, part)
        return copy(block, block, dn_s.at[part, d, j], dn_r.at[part, d, j], below)

    def up_arrived(part, d, j):
        block = ring_block(y - d - 1, j, part)
        copy(
            block, block, up_s.at[part, d, j], up_r.at[part, d, j], above
        ).wait_recv()

    def down_arrived(part, d, j):
        block = ring_block(y + d + 1, j, part)
        copy(
            block, block, dn_s.at[part, d, j], dn_r.at[part, d, j], below
        ).wait_recv()

    def first_step(j, carry):
        block = wbuf.at[y, place(j)]
        copy(block, block, s1_s.at[away(j)], s1_r.at[away(j)], above).wait_recv()
        up_copy(0, 0, j).start()
        down_copy(0, 0, j).start()
        return carry

    def first_steps(low, high):
        lax.fori_loop(low, high, first_step, 0)

    def first_own():
        up_copy(0, 0, 0).start()
        down_copy(0, 0, 0).start()

    @pl.when(mix == 0)
    def _():
        first_own()

    for load in loads[3:]:
        load.wait()
    id0, id1 = ids_v[0:1], ids_v[1:2]
    n_tok = id0.shape[1]
    names = lax.broadcasted_iota(jnp.int32, (16, n_tok), 0)
    named = jnp.where((names == id0) | (names == id1), 1.0, 0.0).astype(BF16)
    row_i = lax.broadcasted_iota(jnp.int32, (n_tok, n_tok), 0)
    col_i = lax.broadcasted_iota(jnp.int32, (n_tok, n_tok), 1)
    before = mm(named, jnp.where(row_i < col_i, 1.0, 0.0).astype(BF16))

    def slot_of(expert):
        rank = jnp.sum(jnp.where(names == expert, before, 0.0), axis=0, keepdims=True)
        k = ((expert >> 1) - z + SIDE) & 3
        f = ((expert >> 3) + x) & 1
        m = (expert + c) & 1
        return (k * 4 + f * 2 + m) * PAIR + rank.astype(jnp.int32)

    slot0, slot1 = slot_of(id0), slot_of(id1)

    def mark(first, count, slot):
        slots = lax.broadcasted_iota(jnp.int32, (count, n_tok), 0) + first
        return jnp.where(slots == slot, 1.0, 0.0)

    def column(row):
        return jnp.transpose(jnp.broadcast_to(row, (n_tok, n_tok)))[:, 0:1]

    r0, r1 = column(rout_v[0:1]), column(rout_v[1:2])
    cot = cot_in[...].astype(F32)
    staged = jnp.concatenate(
        [tok[...], (r0 * cot).astype(BF16), (r1 * cot).astype(BF16)], axis=0
    )

    quarter = BLOCKS * PAIR // 4

    def pack(part):
        first = part * quarter
        m0, m1 = mark(first, quarter, slot0), mark(first, quarter, slot1)
        g0 = mark(first, quarter, slot0 + CAP)
        g1 = mark(first, quarter, slot1 + CAP)
        chosen = jnp.concatenate(
            [(m0 + m1).astype(BF16), g0.astype(BF16), g1.astype(BF16)], axis=1
        )
        sendb[pl.ds(first, quarter)] = mm(chosen, staged).astype(BF16)
        for i in ORDER:
            if i // 4 == part:
                here = pl.ds(i * PAIR, PAIR)
                copy(
                    sendb.at[here], recv.at[here], d_s.at[i], d_r.at[i], target(i)
                ).start()

    @pl.when(mix == 0)
    def _():
        first_steps(1, 3)

    pack(2)
    swap.wait_recv()
    row_sends(1)

    @pl.when(mix == 1)
    def _():
        first_own()

    @pl.when(mix == 0)
    def _():
        first_steps(3, 5)

    pack(1)

    @pl.when(mix == 0)
    def _():
        first_steps(5, 7)

    pack(3)

    @pl.when(mix == 1)
    def _():
        first_steps(1, 3)

    pack(0)
    recv[pl.ds(0, PAIR)] = sendb[pl.ds(0, PAIR)]

    @pl.when(mix == 0)
    def _():
        first_steps(7, SIDE)

    @pl.when(mix == 1)
    def _():
        first_steps(3, SIDE)

    half = SIDE // 2

    def onward(part, d):
        def step(j, carry):
            up_arrived(part, d - 1, j)
            up_copy(part, d, j).start()
            down_arrived(part, d - 1, j)
            down_copy(part, d, j).start()
            return carry

        lax.fori_loop(0, SIDE, step, 0)

    def onward_last(part):
        def step(j, carry):
            up_arrived(part, 2, j)
            up_copy(part, 3, j).start()
            down_arrived(part, 2, j)
            up_arrived(part, 2, j + half)
            down_arrived(part, 2, j + half)
            down_copy(part, 3, j + half).start()
            return carry

        lax.fori_loop(0, half, step, 0)

    def landed(part):
        def step(j, carry):
            up_arrived(part, 3, j)
            down_arrived(part, 3, j + half)
            return carry

        lax.fori_loop(0, half, step, 0)

    def down_first(j, carry):
        up_copy(1, 0, j).start()
        down_copy(1, 0, j).start()
        return carry

    onward(0, 1)
    lax.fori_loop(0, SIDE, down_first, 0)
    onward(0, 2)
    onward(1, 1)
    onward_last(0)
    onward(1, 2)

    for i in ORDER:
        here = pl.ds(i * PAIR, PAIR)
        copy(sendb.at[here], recv.at[here], d_s.at[i], d_r.at[i], target(i)).wait_recv()
    for i in range(0, BLOCKS, 2):
        both = recv[pl.ds(i * PAIR, 2 * PAIR)].astype(F32)
        here = pl.ds(i * CAP, 2 * CAP)
        xs[here] = jnp.concatenate(
            [both[0:CAP], both[PAIR : PAIR + CAP]], axis=0
        ).astype(BF16)
        gs[here] = jnp.concatenate(
            [both[CAP:PAIR], both[PAIR + CAP : 2 * PAIR]], axis=0
        ).astype(BF16)

    depth = SIDE * SHARD

    def accumulate(part, shifts, start):
        blocks = [wrap(y + s) for s in shifts]
        cols = [pl.ds(pl.multiple_of(b * depth, depth), depth) for b in blocks]
        rows = gs if part else xs
        rows = jnp.concatenate([rows[:, at] for at in cols], axis=1)
        for which in (2,) if part else (0, 1):
            held = jnp.concatenate(
                [wbuf[b, :, which].reshape(depth, FF) for b in blocks], axis=0
            )
            term = mm(rows, held)
            acc[which] = term if start else acc[which] + term

    def accumulate_near(part):
        accumulate(part, (0, 1), True)
        accumulate(part, (-1, 2), False)
        accumulate(part, (-2, 3), False)
        accumulate(part, (-3,), False)

    accumulate_near(0)
    onward_last(1)
    gst[...] = jnp.transpose(gs[...])
    landed(0)
    accumulate(0, (4,), False)

    def weight(which):
        return wbuf[:, :, which].reshape(WIDTH, FF)

    gate, up = acc[0], acc[1]
    sig = jax.nn.sigmoid(gate)
    act = gate * sig
    hidden = (act * up).astype(BF16)

    dw = mm(gst[...], hidden).astype(BF16)
    dwy[...] = dw[:, 0:WIDE].reshape(SIDE, SIDE * SHARD, WIDE)
    dwx[...] = dw[:, WIDE:FF].reshape(SIDE, SIDE, SHARD, FF - WIDE)

    def y1_copy(o):
        to = wrap(y + o)
        return copy(dwy.at[to], ry1.at[o], y1_s.at[o], y1_r.at[o], {"y": to})

    def x1_copy(o):
        to = wrap(x + o)
        return copy(dwx.at[:, to], rx1.at[o], x1_s.at[o], x1_r.at[o], {"x": to})

    for o in (4, 3, 5, 2, 6, 1, 7):
        y1_copy(o).start()
        x1_copy(o).start()

    accumulate_near(1)
    for k in range(3):
        whole = (
            mark(0, BLOCKS * PAIR, slot0)
            if k == 0
            else mark(0, BLOCKS * PAIR, slot1)
            if k == 1
            else mark(0, BLOCKS * PAIR, slot0 + CAP)
            + mark(0, BLOCKS * PAIR, slot1 + CAP)
        )
        back_mark[pl.ds(k * n_tok, n_tok)] = jnp.transpose(whole).astype(BF16)
    landed(1)
    accumulate(1, (4,), False)
    gate_w, up_w, down_w = weight(0), weight(1), weight(2)
    hid_grad = acc[2]
    gate_grad = (hid_grad * up * (sig * (1.0 + gate * (1.0 - sig)))).astype(BF16)
    up_grad = (hid_grad * act).astype(BF16)

    def result_copy(i):
        here = pl.ds(i * PAIR, PAIR)
        return copy(outb.at[here], back.at[here], b_s.at[i], b_r.at[i], origin(i))

    part_rows = 4 * CAP
    for part in (2, 1, 3, 0):
        rows = slice(part * part_rows, (part + 1) * part_rows)
        made = mm_nt(hidden[rows], down_w)
        grad = mm_nt(gate_grad[rows], gate_w) + mm_nt(up_grad[rows], up_w)
        pieces = []
        for j in range(4):
            pieces.append(made[j * CAP : (j + 1) * CAP])
            pieces.append(grad[j * CAP : (j + 1) * CAP])
        outb[pl.ds(part * 4 * PAIR, 4 * PAIR)] = jnp.concatenate(pieces, axis=0).astype(
            BF16
        )
        for i in ORDER:
            if i // 4 == part:
                result_copy(i).start()
    back[pl.ds(0, PAIR)] = outb[pl.ds(0, PAIR)]

    total = dwy[y].astype(F32)
    for o in (1, 7, 2, 6, 3, 5, 4):
        y1_copy(o).wait_recv()
        total = total + ry1[o].astype(F32)
    sy1[...] = total.astype(BF16).reshape(SIDE, SHARD, WIDE)

    own_plane = wrap(z + 4 * mix)

    def y2_copy(o):
        to = wrap(x + o)
        slot = 2 * (o // 2) + mix
        return copy(
            sy1.at[to],
            ry2.at[slot],
            y2_s.at[o],
            y2_r.at[slot],
            {"x": to, "z": own_plane},
        )

    y2_copy_self = y2_copy(0)

    @pl.when(mix == 0)
    def _():
        ry2[0] = sy1[x]

    @pl.when(mix == 1)
    def _():
        y2_copy_self.start()

    for o in (4, 3, 5, 2, 6, 1, 7):
        y2_copy(o).start()

    same = dwx[:, x].astype(F32)
    other = None
    for o in (1, 7, 2, 6, 3, 5, 4):
        x1_copy(o).wait_recv()
        term = rx1[o].astype(F32)
        if o % 2 == 0:
            same = same + term
        else:
            other = term if other is None else other + term
    sx1[0] = same.astype(BF16)
    sx1[1] = other.astype(BF16)

    def x2_copy(which, o):
        to = wrap(y + o)
        held = lax.rem(mix + which, 2)
        return copy(
            sx1.at[held, to],
            rx2.at[which, o],
            x2_s.at[which, o],
            x2_r.at[which, o],
            {"y": to, "z": wrap(z + 4 * which)},
        )

    rx2[0, 0] = sx1[mix, y]
    x2_copy(1, 0).start()
    for o in (4, 3, 5, 2, 6, 1, 7):
        x2_copy(0, o).start()
        x2_copy(1, o).start()

    for i in ORDER:
        result_copy(i).wait_recv()
    from_mark = mm(back_mark[...], back[...])
    out_ref[...] = (r0 * from_mark[0:n_tok] + r1 * from_mark[n_tok : 2 * n_tok]).astype(
        BF16
    )
    tg_ref[...] = from_mark[2 * n_tok : 3 * n_tok].astype(BF16)

    def y2_arrived(slot):
        copy(
            sy1.at[0], ry2.at[slot], y2_s.at[0], y2_r.at[slot], {"z": own_plane}
        ).wait_recv()

    @pl.when(mix == 1)
    def _():
        y2_arrived(0)

    for slot in range(1, SIDE):
        y2_arrived(slot)
    for o in range(SIDE):
        for which in (0, 1):
            if o or which:
                x2_copy(which, o).wait_recv()
    scale = 1.0 / (SIDE * SIDE)
    wide = ry2[0].astype(F32)
    for slot in range(1, SIDE):
        wide = wide + ry2[slot].astype(F32)
    narrow = None
    for o in range(SIDE):
        for which in (0, 1):
            term = rx2[which, o].astype(F32)
            narrow = term if narrow is None else narrow + term
    dg_ref[0] = jnp.concatenate([wide, narrow], axis=1) * scale

    swap.wait_send()
    for which in (0, 1):
        for i in range(4):
            off, sent = row_copy(which, i)
            if i == 0:

                @pl.when(off != 0)
                def _():
                    sent.wait_send()
            else:
                sent.wait_send()
    for part in (0, 1):
        for d in (0, 1, 2):

            def drained(j, carry, part=part, d=d):
                up_copy(part, d, j).wait_send()
                down_copy(part, d, j).wait_send()
                return carry

            lax.fori_loop(0, SIDE, drained, 0)

        def drained_last(j, carry, part=part):
            up_copy(part, 3, j).wait_send()
            down_copy(part, 3, j + half).wait_send()
            return carry

        lax.fori_loop(0, half, drained_last, 0)
    for i in ORDER:
        here = pl.ds(i * PAIR, PAIR)
        copy(sendb.at[here], recv.at[here], d_s.at[i], d_r.at[i], target(i)).wait_send()
        result_copy(i).wait_send()

    @pl.when(mix == 1)
    def _():
        y2_copy_self.wait_send()

    x2_copy(1, 0).wait_send()
    for o in range(1, SIDE):
        y1_copy(o).wait_send()
        x1_copy(o).wait_send()
        y2_copy(o).wait_send()
        x2_copy(0, o).wait_send()
        x2_copy(1, o).wait_send()


def store(out_v, tg_v, dg_v, out_ref, tg_ref, dg_ref, sem):
    moves = [
        pltpu.make_async_copy(src, dst, sem.at[n])
        for n, (src, dst) in enumerate(
            ((out_v, out_ref), (tg_v, tg_ref), (dg_v, dg_ref))
        )
    ]
    for move in moves:
        move.start()
    for move in moves:
        move.wait()


def local(tokens, expert_ids, routing, w_gate, w_up, w_down, grad_out):
    n_tok = tokens.shape[0]
    vmem = pl.BlockSpec(memory_space=pltpu.VMEM)
    hbm = pl.BlockSpec(memory_space=pltpu.HBM)
    dma = pltpu.SemaphoreType.DMA
    narrow = FF - WIDE
    made = pl.pallas_call(
        kernel,
        out_shape=(
            jax.ShapeDtypeStruct((n_tok, WIDTH), BF16),
            jax.ShapeDtypeStruct((n_tok, WIDTH), BF16),
            jax.ShapeDtypeStruct((1, SHARD, FF), F32),
        ),
        in_specs=[hbm] * 7,
        out_specs=(vmem, vmem, vmem),
        scratch_shapes=[
            pltpu.VMEM((n_tok, WIDTH), BF16),
            pltpu.VMEM((n_tok, WIDTH), BF16),
            pltpu.VMEM((2, n_tok), jnp.int32),
            pltpu.VMEM((2, n_tok), F32),
            pltpu.VMEM((2, 3, SHARD, FF), BF16),
            pltpu.VMEM((SIDE, SIDE, 3, SHARD, FF), BF16),
            pltpu.VMEM((BLOCKS * PAIR, WIDTH), BF16),
            pltpu.VMEM((BLOCKS * PAIR, WIDTH), BF16),
            pltpu.VMEM((ROWS, WIDTH), BF16),
            pltpu.VMEM((ROWS, WIDTH), BF16),
            pltpu.VMEM((WIDTH, ROWS), BF16),
            pltpu.VMEM((3, ROWS, FF), F32),
            pltpu.VMEM((BLOCKS * PAIR, WIDTH), BF16),
            pltpu.VMEM((BLOCKS * PAIR, WIDTH), BF16),
            pltpu.VMEM((SIDE, SIDE * SHARD, WIDE), BF16),
            pltpu.VMEM((SIDE, SIDE * SHARD, WIDE), BF16),
            pltpu.VMEM((SIDE, SHARD, WIDE), BF16),
            pltpu.VMEM((SIDE, SHARD, WIDE), BF16),
            pltpu.VMEM((SIDE, SIDE, SHARD, narrow), BF16),
            pltpu.VMEM((SIDE, SIDE, SHARD, narrow), BF16),
            pltpu.VMEM((2, SIDE, SHARD, narrow), BF16),
            pltpu.VMEM((2, SIDE, SHARD, narrow), BF16),
            pltpu.VMEM((3 * n_tok, BLOCKS * PAIR), BF16),
            dma((7,)),
            dma,
            dma,
            dma((SIDE,)),
            dma((SIDE,)),
            dma((2, 4, SIDE)),
            dma((2, 4, SIDE)),
            dma((2, 4, SIDE)),
            dma((2, 4, SIDE)),
            dma((BLOCKS,)),
            dma((BLOCKS,)),
            dma((BLOCKS,)),
            dma((BLOCKS,)),
            dma((SIDE,)),
            dma((SIDE,)),
            dma((SIDE,)),
            dma((SIDE,)),
            dma((SIDE,)),
            dma((SIDE,)),
            dma((2, SIDE)),
            dma((2, SIDE)),
        ],
        compiler_params=pltpu.CompilerParams(
            collective_id=0,
            has_side_effects=True,
            vmem_limit_bytes=44 * 1024 * 1024,
        ),
        cost_estimate=pl.CostEstimate(
            flops=3_000_000_000, bytes_accessed=2_000_000, transcendentals=150_000
        ),
    )(
        *(
            pltpu.with_memory_space_constraint(a, pltpu.HBM)
            for a in (
                tokens,
                expert_ids.T,
                routing.T,
                w_gate,
                w_up,
                w_down,
                grad_out,
            )
        )
    )
    return pl.pallas_call(
        store,
        out_shape=[jax.ShapeDtypeStruct(a.shape, a.dtype) for a in made],
        in_specs=[vmem] * 3,
        out_specs=[hbm] * 3,
        scratch_shapes=[dma((3,))],
        compiler_params=pltpu.CompilerParams(vmem_limit_bytes=1024 * 1024),
    )(*made)


def solution(mesh):
    finer = Mesh(mesh.devices.reshape(SIDE, SIDE, SIDE, 2), ("y", "x", "z", "c"))
    every = ("y", "x", "z", "c")
    rows = P(every, None)
    weights = P(("z", "c"), ("y", "x"), None)
    return jax.shard_map(
        local,
        mesh=finer,
        in_specs=(rows, rows, rows, weights, weights, weights, rows),
        out_specs=(rows, rows, weights),
        check_vma=False,
    )
```
